256 devices in a mesh: ctx: 64 (over z, y, core), head: 4 (over x).
Axes of the slice: x: 4, y: 4, z: 8, core: 2. Of those that a mesh axis runs over, the one named last changes fastest.
Arguments:
- queries: bfloat16 [1, 8192, 2048], P(None, 'ctx', 'head'), may hold values from -24 to 24
- keys: bfloat16 [8192, 512], P('ctx', 'head'), may hold values from -6 to 6
- values: bfloat16 [8192, 512], P('ctx', 'head'), may hold values from -6 to 6
- query_pos: int32 [8192], P('ctx'), may hold values from 0 to 8191, as said below
- cot_out: bfloat16 [1, 8192, 4096], P(None, 'ctx'), may hold values from -6 to 6
- out_weight: bfloat16 [1, 2048, 4096], P(None, 'head'), may hold values from -0.09375 to 0.09375
Outputs:
- grad_queries: bfloat16 [1, 8192, 2048], P(None, 'ctx', 'head')
- grad_keys: float32 [8192, 512], P('ctx', 'head')
- grad_values: float32 [8192, 512], P('ctx', 'head')
The draws below stay inside these ranges and needn't reach their ends.
Inputs may be any that keep to these rules, and one draw needn't show every extreme that they name: `query_pos`: the 128 rows of each index of ctx hold the consecutive positions t * 128 to t * 128 + 127 in order, and the tiles t of all indices of ctx are a permutation.
All inputs are finite; a program needn't handle non-finite values.
Results may differ from the reference program's by a relative error of at most 0.0057.
Values may be sent and summed in bfloat16 or wider, within the bound.
A program may use at most 128 MiB of HBM per device.

```python
import jax
import jax.numpy as jnp
from jax import lax

D = 4096
HEADS = 16
KV_HEADS = 4
HEAD_DIM = 128
LAYERS = 1
TOK_DEV = 128
TOKENS = 8192


def tile_positions(key):
    tile_count = TOKENS // TOK_DEV
    order = jax.random.permutation(jax.random.fold_in(key, 11), tile_count)
    return (order[:, None] * TOK_DEV + jnp.arange(TOK_DEV)[None, :]).reshape(-1).astype(jnp.int32)


def draw_query_pos(key, part):
    return tile_positions(key)


def draw_keys(key, part):
    key = jax.random.fold_in(key, 3)
    result = jnp.clip(jax.random.normal(key, (TOKENS, KV_HEADS * HEAD_DIM), jnp.float32), -6.0, 6.0)
    return result.astype(jnp.bfloat16)


def draw_queries(key, part):
    key = jax.random.fold_in(key, 5)
    shape = (LAYERS, TOKENS, HEADS * HEAD_DIM)
    result = jnp.clip(jax.random.normal(key, shape, jnp.float32), -6.0, 6.0)
    return result.astype(jnp.bfloat16)


def level_of(key, shape, pieces, least, top_value):
    def one(dim, shards_of):
        draws = jax.random.uniform(jax.random.fold_in(jax.random.fold_in(key, 6), dim), (shards_of,), jnp.float32, least / len(pieces), top_value / len(pieces))
        return jnp.repeat(jnp.exp(draws), shape[dim] // shards_of).reshape((-1,) + (1,) * (len(shape) - dim - 1))

    factor_of = one(*pieces[0])
    for cut in pieces[1:]:
        factor_of = factor_of * one(*cut)
    return factor_of


def bell_draw(key, extent, deviation, reach, pieces=(), kind=jnp.bfloat16):
    values = jax.random.normal(key, extent, jnp.float32) * deviation
    if len(pieces) > 0:
        values = level_of(key, extent, pieces, -0.22, 0.18) * values
    return jnp.clip(values, min=-reach, max=reach).astype(kind)


def setup_inputs(seed: int = 0) -> dict:
    key_of = jax.random.split(jax.random.key(seed), 7)
    queries = draw_queries(jax.random.fold_in(key_of[6], 71), 0)
    keys = draw_keys(jax.random.fold_in(key_of[6], 71), 0)
    values = bell_draw(key_of[2], (TOKENS, KV_HEADS * HEAD_DIM), 1.0, 6.0, ((0, 64), (1, 4)))
    query_pos = draw_query_pos(jax.random.fold_in(key_of[6], 71), 0)
    cot_out = bell_draw(key_of[4], (LAYERS, TOKENS, D), 1.0, 6.0, ((1, 64),))
    out_weight = bell_draw(key_of[5], (LAYERS, HEADS * HEAD_DIM, D), D ** -0.5, 0.09375, ((1, 4),))
    return {"queries": queries, "keys": keys, "values": values, "query_pos": query_pos, "cot_out": cot_out, "out_weight": out_weight}


def head_terms(query_head, key_head, value_head, dout_head, visible):
    score_scale = HEAD_DIM ** -0.5
    score = jnp.dot(query_head, key_head.T, preferred_element_type=jnp.float32) * score_scale
    score = jnp.where(visible, score, -jnp.inf)
    row_top = jnp.max(score, axis=1, keepdims=True)
    log_total = row_top + jnp.log(jnp.sum(jnp.exp(score - row_top), axis=1, keepdims=True))
    prob = jnp.exp(score - log_total)
    grad_prob = jnp.dot(dout_head, value_head.T, preferred_element_type=jnp.float32)
    delta = jnp.sum(prob * grad_prob, axis=1, keepdims=True)
    grad_score = (prob * (grad_prob - delta)).astype(jnp.bfloat16)
    prob_low = prob.astype(jnp.bfloat16)
    grad_query = (jnp.dot(grad_score, key_head, preferred_element_type=jnp.float32) * score_scale).astype(jnp.bfloat16)
    grad_key = jnp.dot(grad_score.T, query_head, preferred_element_type=jnp.float32) * score_scale
    grad_value = jnp.dot(prob_low.T, dout_head, preferred_element_type=jnp.float32)
    return grad_query, grad_key, grad_value


def reference(queries, keys, values, query_pos, cot_out, out_weight):
    group_size = HEADS // KV_HEADS
    visible = jnp.arange(TOKENS, dtype=jnp.int32)[None, :] <= query_pos[:, None]
    query_grads = []
    key_total = jnp.zeros((TOKENS, KV_HEADS * HEAD_DIM), jnp.float32)
    value_total = jnp.zeros((TOKENS, KV_HEADS * HEAD_DIM), jnp.float32)
    for layer in range(LAYERS):
        dout_all = jnp.dot(cot_out[layer], out_weight[layer].T, preferred_element_type=jnp.float32).astype(jnp.bfloat16)
        layer_queries = queries[layer]

        def one_head(head_index):
            kv_index = head_index // group_size
            query_head = lax.dynamic_slice_in_dim(layer_queries, head_index * HEAD_DIM, HEAD_DIM, 1)
            dout_head = lax.dynamic_slice_in_dim(dout_all, head_index * HEAD_DIM, HEAD_DIM, 1)
            key_head = lax.dynamic_slice_in_dim(keys, kv_index * HEAD_DIM, HEAD_DIM, 1)
            value_head = lax.dynamic_slice_in_dim(values, kv_index * HEAD_DIM, HEAD_DIM, 1)
            return head_terms(query_head, key_head, value_head, dout_head, visible)

        grad_query, grad_key, grad_value = lax.map(one_head, jnp.arange(HEADS, dtype=jnp.int32))
        query_grads.append(grad_query.transpose(1, 0, 2).reshape(TOKENS, HEADS * HEAD_DIM))
        key_total = key_total + grad_key.reshape(KV_HEADS, group_size, TOKENS, HEAD_DIM).sum(axis=1).transpose(1, 0, 2).reshape(TOKENS, KV_HEADS * HEAD_DIM)
        value_total = value_total + grad_value.reshape(KV_HEADS, group_size, TOKENS, HEAD_DIM).sum(axis=1).transpose(1, 0, 2).reshape(TOKENS, KV_HEADS * HEAD_DIM)
    return jnp.stack(query_grads), key_total, value_total
```

```python
import jax
import jax.numpy as jnp
import numpy as np
from jax import lax
from jax.experimental import pallas as pl
from jax.experimental.pallas import tpu as pltpu
from jax.sharding import PartitionSpec as P

HEAD_DIM = 128
GROUP = 4
TILE = 128
ZS, YS, CORES = 8, 4, 2
CHUNK = CORES * TILE
ROWS = YS * TILE
MODEL = 4096
SCALE = HEAD_DIM**-0.5
SCALE_LOG2 = float(SCALE * np.log2(np.e))
HIDDEN = -1e30
FLOOR = -1e20
BF, F32, I32 = jnp.bfloat16, jnp.float32, jnp.int32
MESH = pl.DeviceIdType.MESH
VM = pltpu.VMEM
COPIES = 80


def nt(a, b):
    return lax.dot_general(a, b, (((1,), (1,)), ((), ())), preferred_element_type=F32)


def nn(a, b):
    return lax.dot_general(a, b, (((1,), (0,)), ((), ())), preferred_element_type=F32)


def tn(a, b):
    return lax.dot_general(a, b, (((0,), (0,)), ((), ())), preferred_element_type=F32)


def kernel(
    q_hbm, k_hbm, v_hbm, pos_hbm, cot_hbm, w_hbm,
    g_ref,
    wbuf, cbuf, pos_s, qbuf, dobuf, kv, tbuf, pst, dpst, mstat, lstat, xstat, st, tot,
    acc, dq_acc, sib_out, sib_in, ring_out, relay_in, near_in, dq_out, dq_in,
    lsem, ssem, rsem,
):
    me = lax.axis_index("ctx")
    core = me % 2
    y = (me // 2) % YS
    z = me // (2 * YS)

    def at(dz=0, dy=0, other=False):
        zz = (z + dz + ZS) % ZS
        yy = (y + dy + YS) % YS
        cc = 1 - core if other else core
        return (zz * YS + yy) * 2 + cc

    zr, zl, yr, yl, yo, sib = at(dz=1), at(dz=-1), at(dy=1), at(dy=-1), at(dy=2), at(other=True)

    used = [0, 0]
    sends = []

    def send(src, dst, dev):
        i = used[0]
        used[0] += 1
        d = pltpu.make_async_remote_copy(
            src_ref=src, dst_ref=dst, send_sem=ssem.at[i], recv_sem=rsem.at[i],
            device_id={"ctx": dev}, device_id_type=MESH,
        )
        d.start()
        sends.append(d)
        return d

    def local(src, dst):
        i = used[1]
        used[1] += 1
        d = pltpu.make_async_copy(src, dst, lsem.at[i])
        d.start()
        return d

    own_kv = [local(k_hbm, kv.at[0, 0, 0]), local(v_hbm, kv.at[0, 0, 1])]
    own_pos = local(pos_hbm, pos_s)
    own_q = [local(q_hbm.at[0, :, pl.ds(h * 128, 128)], qbuf.at[h, 0]) for h in range(GROUP)]
    own_c = local(cot_hbm.at[0], cbuf)
    own_w = [local(w_hbm.at[0, pl.ds(i * 256, 256)], wbuf.at[i]) for i in range(2)]

    barrier = pltpu.get_barrier_semaphore()
    greeted = (zr, zl, at(dz=2), at(dz=-2), yr, yl, yo, sib)
    for dev in greeted:
        pl.semaphore_signal(barrier, inc=1, device_id={"ctx": dev}, device_id_type=MESH)

    own_c.wait()
    for i in range(2):
        own_w[i].wait()
        out = nt(cbuf[...], wbuf[i])
        for j in range(2):
            dobuf[2 * i + j, 0] = out[:, j * 128 : (j + 1) * 128].astype(BF)
    for d in own_kv + own_q:
        d.wait()
    own_pos.wait()
    tbuf[0] = jnp.full((8, 128), pos_s[0], I32)
    pl.semaphore_wait(barrier, len(greeted))

    def to_y(src, dst):
        return [send(src, dst(3), yr), send(src, dst(1), yl), send(src, dst(2), yo)]

    kv_sib = {0: send(kv.at[0, 0], kv.at[0, 1], sib)}
    kv_in = {
        7: [send(kv.at[0, 0], kv.at[7, 0], zr)],
        1: [send(kv.at[0, 0], kv.at[1, 0], zl)],
        6: [send(kv.at[0, 0], kv.at[6, 0], at(dz=2))],
        2: [send(kv.at[0, 0], kv.at[2, 0], at(dz=-2))],
    }
    t_in = to_y(tbuf.at[0], lambda n: tbuf.at[n])
    q_in = to_y(qbuf.at[:, 0], lambda n: qbuf.at[:, n])
    do_in = to_y(dobuf.at[:, 0], lambda n: dobuf.at[:, n])

    def arrive(n):
        for d in kv_in[n]:
            d.wait_recv()
        kv_sib[n] = send(kv.at[n, 0], kv.at[n, 1], sib)

    def relay():
        arrive(6)
        kv_in[5] = [send(kv.at[6, 0], kv.at[5, 0], zr)]
        kv_in[4] = [send(kv.at[6, 0, 0], kv.at[4, 0, 0], at(dz=2))]
        arrive(2)
        kv_in[3] = [send(kv.at[2, 0], kv.at[3, 0], zl)]
        kv_in[4].append(send(kv.at[2, 0, 1], kv.at[4, 0, 1], at(dz=-2)))

    lane = lax.broadcasted_iota(I32, (1, 128), 1)
    krow = lax.broadcasted_iota(I32, (TILE, 128), 0)

    def stat_row(h, dy):
        return ((y + dy) % YS) * GROUP + h

    def score_pass(dz):
        base = [(((z + dz) % ZS * YS + y) * 2 + c) * TILE for c in (core, 1 - core)]

        def step(h, _):
            keys = kv[dz, :, 0].reshape(CHUNK, HEAD_DIM)
            s = nt(keys, qbuf[h].reshape(ROWS, HEAD_DIM))
            for dy in range(YS):
                pos = tbuf[dy][0:1, :] + lane
                parts = []
                for c in range(2):
                    part = s[c * TILE : (c + 1) * TILE, dy * 128 : (dy + 1) * 128] * SCALE_LOG2
                    parts.append(jnp.where(krow <= pos - base[c], part, HIDDEN))
                top = jnp.maximum(
                    jnp.max(jnp.maximum(parts[0], parts[1]), axis=0, keepdims=True), FLOOR
                )
                total = jnp.zeros((TILE, 128), F32)
                for c in range(2):
                    e = jnp.exp2(parts[c] - top)
                    pst[dz, h, c * TILE : (c + 1) * TILE, dy * 128 : (dy + 1) * 128] = e
                    total = total + e
                row = stat_row(h, dy)
                mstat[dz, pl.ds(row, 1), :] = top
                lstat[dz, pl.ds(row, 1), :] = jnp.sum(total, axis=0, keepdims=True)
            return 0

        for h in range(GROUP):
            step(h, 0)

    def cross_pass(dz):
        def step(h, _):
            vals = kv[dz, :, 1].reshape(CHUNK, HEAD_DIM)
            dp = nt(vals, dobuf[h].reshape(ROWS, HEAD_DIM))
            dpst[dz, h] = dp
            cross = jnp.sum(dp * pst[dz, h], axis=0, keepdims=True)
            for dy in range(YS):
                xstat[dz, pl.ds(stat_row(h, dy), 1), :] = cross[:, dy * 128 : (dy + 1) * 128]
            return 0

        for h in range(GROUP):
            step(h, 0)

    for n in (1, 7):
        arrive(n)
    for d in q_in + t_in:
        d.wait_recv()
    kv_sib[0].wait_recv()
    relay()
    score_pass(0)
    for n in (1, 7, 2, 6):
        kv_sib[n].wait_recv()
        score_pass(n)
    for d in do_in:
        d.wait_recv()
    for n in (0, 1, 7):
        cross_pass(n)
    arrive(3)
    arrive(5)
    cross_pass(2)
    cross_pass(6)
    for n in (3, 5):
        kv_sib[n].wait_recv()
        score_pass(n)
    arrive(4)
    cross_pass(3)
    cross_pass(5)
    kv_sib[4].wait_recv()
    score_pass(4)
    cross_pass(4)

    top = mstat[0]
    for i in range(1, ZS):
        top = jnp.maximum(top, mstat[i])
    total, cross = jnp.zeros_like(top), jnp.zeros_like(top)
    for i in range(ZS):
        w = jnp.exp2(mstat[i] - top)
        total = total + lstat[i] * w
        cross = cross + xstat[i] * w
    st[0, 0], st[0, 1], st[0, 2] = top, total, cross
    for d in to_y(st.at[0], lambda n: st.at[n]):
        d.wait_recv()
    top = jnp.maximum(jnp.maximum(st[0, 0], st[1, 0]), jnp.maximum(st[2, 0], st[3, 0]))
    total, cross = jnp.zeros_like(top), jnp.zeros_like(top)
    for i in range(YS):
        w = jnp.exp2(st[i, 0] - top)
        total = total + st[i, 1] * w
        cross = cross + st[i, 2] * w
    tot[0] = top + jnp.log2(total)
    tot[1] = cross / total

    def grad_pass(dz, heads, first, dq_first):
        keys = kv[dz, :, 0].reshape(CHUNK, HEAD_DIM)
        dk, dv = [], []
        for h in heads:
            rows = [stat_row(h, dy) for dy in range(YS)]
            factor = jnp.concatenate(
                [jnp.exp2(mstat[dz, pl.ds(r, 1), :] - tot[0, pl.ds(r, 1), :]) for r in rows], axis=1
            )
            delta = jnp.concatenate([tot[1, pl.ds(r, 1), :] for r in rows], axis=1)
            prob = pst[dz, h] * factor
            ds = (prob * (dpst[dz, h] - delta)).astype(BF)
            prob = prob.astype(BF)
            dv_now = nn(prob, dobuf[h].reshape(ROWS, HEAD_DIM))
            dk_now = nn(ds, qbuf[h].reshape(ROWS, HEAD_DIM))
            if first and h == heads[0]:
                acc[dz, 0], acc[dz, 1] = dk_now, dv_now
            else:
                acc[dz, 0] += dk_now
                acc[dz, 1] += dv_now
            dq = tn(keys, ds)
            if dq_first:
                dq_acc[h] = dq
            else:
                dq_acc[h] += dq

    sib_copies = {}

    def to_sib(dz):
        for i in range(2):
            sib_out[dz, i] = acc[dz, i, TILE:].astype(BF)
        sib_copies[dz] = send(sib_out.at[dz], sib_in.at[dz], sib)

    def pair(dz):
        sib_copies[dz].wait_recv()
        return [acc[dz, i, :TILE] + sib_in[dz, i].astype(F32) for i in range(2)]

    def to_owner(dz, parts):
        ring_out[dz, 0], ring_out[dz, 1] = parts[0].astype(BF), parts[1].astype(BF)

    every = tuple(range(GROUP))
    grad_pass(4, every, True, True)
    to_sib(4)
    grad_pass(3, every, True, False)
    to_sib(3)
    to_owner(4, pair(4))
    far = [
        send(ring_out.at[4, 0], relay_in.at[0, 0], at(dz=2)),
        send(ring_out.at[4, 1], relay_in.at[1, 1], at(dz=-2)),
    ]
    grad_pass(5, every, True, False)
    to_sib(5)
    to_owner(3, pair(3))
    three = [send(ring_out.at[3], relay_in.at[2], zr)]
    rest = (2, 6, 1, 7, 0)
    for n in rest:
        grad_pass(n, (0, 1), True, False)
        if n == 2:
            to_owner(5, pair(5))
            three.append(send(ring_out.at[5], relay_in.at[3], zl))

    def send_dq(half):
        for dy in range(1, YS):
            for h in half:
                dq_out[dy, h] = dq_acc[h, :, dy * 128 : (dy + 1) * 128].astype(BF)
        cut = pl.ds(half[0], 2)
        return [
            send(dq_out.at[2, cut], dq_in.at[2, cut], yo),
            send(dq_out.at[1, cut], dq_in.at[3, cut], yr),
            send(dq_out.at[3, cut], dq_in.at[1, cut], yl),
        ]

    dq_copies = send_dq((0, 1))
    for n in rest:
        grad_pass(n, (2, 3), False, False)
        to_sib(n)
        if n == 6:
            for d in far + three:
                d.wait_recv()
            gk, gv = pair(2)
            to_owner(2, (gk + relay_in[0, 0].astype(F32) + relay_in[2, 0].astype(F32), gv + relay_in[2, 1].astype(F32)))
            near = [send(ring_out.at[2], near_in.at[0], at(dz=2))]
        if n == 1:
            gk, gv = pair(6)
            to_owner(6, (gk + relay_in[3, 0].astype(F32), gv + relay_in[1, 1].astype(F32) + relay_in[3, 1].astype(F32)))
            near.append(send(ring_out.at[6], near_in.at[1], at(dz=-2)))
        if n == 7:
            to_owner(1, pair(1))
            near.append(send(ring_out.at[1], near_in.at[2], zr))
    dq_copies += send_dq((2, 3))
    to_owner(7, pair(7))
    near.append(send(ring_out.at[7], near_in.at[3], zl))
    gk, gv = pair(0)
    for d in near:
        d.wait_recv()
    for i in range(4):
        gk = gk + near_in[i, 0].astype(F32)
        gv = gv + near_in[i, 1].astype(F32)
    g_ref[4] = gk * SCALE
    g_ref[5] = gv
    for d in dq_copies:
        d.wait_recv()
    for h in range(GROUP):
        g = dq_acc[h, :, 0:128]
        for n in range(1, YS):
            g = g + dq_in[n, h].astype(F32)
        g_ref[h] = g * SCALE

    for d in sends:
        d.wait_send()
    assert used[0] <= COPIES and used[1] <= 16


def write_out(g_ref, gq_ref, gk_ref, gv_ref):
    for h in range(GROUP):
        gq_ref[0, :, h * 128 : (h + 1) * 128] = g_ref[h].T.astype(BF)
    gk_ref[...] = g_ref[4]
    gv_ref[...] = g_ref[5]


def body(queries, keys, values, query_pos, cot_out, out_weight):
    any_ = pl.BlockSpec(memory_space=pl.ANY)
    vm = pl.BlockSpec(memory_space=VM)
    stat = VM((ZS, YS * GROUP, 128), F32)
    tile = (TILE, 128)
    sums = pl.pallas_call(
        kernel,
        out_shape=jax.ShapeDtypeStruct((6,) + tile, F32),
        in_specs=[any_] * 6,
        out_specs=vm,
        scratch_shapes=[
            VM((2, 256, MODEL), BF),
            VM((TILE, MODEL), BF),
            pltpu.SMEM((TILE,), I32),
            VM((GROUP, YS) + tile, BF),
            VM((GROUP, YS) + tile, BF),
            VM((ZS, 2, 2) + tile, BF),
            VM((YS, 8, 128), I32),
            VM((ZS, GROUP, CHUNK, ROWS), F32),
            VM((ZS, GROUP, CHUNK, ROWS), F32),
            stat, stat, stat,
            VM((YS, 3, YS * GROUP, 128), F32),
            VM((2, YS * GROUP, 128), F32),
            VM((ZS, 2, CHUNK, HEAD_DIM), F32),
            VM((GROUP, HEAD_DIM, ROWS), F32),
            VM((ZS, 2) + tile, BF),
            VM((ZS, 2) + tile, BF),
            VM((ZS, 2) + tile, BF),
            VM((4, 2) + tile, BF),
            VM((4, 2) + tile, BF),
            VM((YS, GROUP) + tile, BF),
            VM((YS, GROUP) + tile, BF),
            pltpu.SemaphoreType.DMA((16,)),
            pltpu.SemaphoreType.DMA((COPIES,)),
            pltpu.SemaphoreType.DMA((COPIES,)),
        ],
        compiler_params=pltpu.CompilerParams(
            collective_id=0, has_side_effects=True, vmem_limit_bytes=60 * 2**20
        ),
    )(queries, keys, values, query_pos, cot_out, out_weight)
    return pl.pallas_call(
        write_out,
        out_shape=(
            jax.ShapeDtypeStruct((1, TILE, GROUP * HEAD_DIM), BF),
            jax.ShapeDtypeStruct(tile, F32),
            jax.ShapeDtypeStruct(tile, F32),
        ),
        in_specs=[vm],
        out_specs=(vm, vm, vm),
    )(sums)


def solution(mesh):
    in_specs = (
        P(None, "ctx", "head"),
        P("ctx", "head"),
        P("ctx", "head"),
        P("ctx"),
        P(None, "ctx", None),
        P(None, "head", None),
    )
    out_specs = (P(None, "ctx", "head"), P("ctx", "head"), P("ctx", "head"))
    return jax.shard_map(body, mesh=mesh, in_specs=in_specs, out_specs=out_specs, check_vma=False)
```
